32 devices in a mesh: dp: 2 (over x), phase: 4 (over z), tensor: 4 (over y, core).
Axes of the slice: x: 2, y: 2, z: 4, core: 2. Of those that a mesh axis runs over, the one named last changes fastest.
Arguments:
- tokens: bfloat16 [2, 512, 8192], P('dp', 'phase', 'tensor'), may hold values from -6 to 6
- bc_proj: bfloat16 [2, 512, 2, 2048], P('dp', 'phase', None, 'tensor'), may hold values from -0.3984375 to 0.3984375
- step_sizes: bfloat16 [2, 64, 1024], P('dp', 'phase', 'tensor'), may hold values from 0.5 to 2
- decay_rates: float32 [128], P('tensor'), may hold values from 0.00024414062 to 0.02
- direct_weight: float32 [128], P('tensor'), may hold values from 0.5 to 1.5
- norm_gain: float32 [8192], P('tensor'), may hold values from 0.1 to 1.9
- routes: int32 [2, 64, 1], P('dp', 'phase'), may hold values from 0 to 1; in each aligned block of 16 rows (0 to 15, 16 to 31, ..., all dimensions but the last counted through in order) at most 16 rows name the same one
- segments: int32 [2, 1024], P('dp', 'phase'), may hold values from 0 to 3, never falling along the last dimension, each value on 1 to 512 neighbouring positions
Outputs:
- mixed: bfloat16 [2, 512, 8192], P('dp', 'phase', 'tensor')
The draws below stay inside these ranges and needn't reach their ends.
Inputs may be any that keep to these rules, and one draw needn't show every extreme that they name: `routes`: no device sends more than 16 of its blocks to one data group. `segments`: document ids never fall along a row; each document covers 1 to 512 positions, and one covers exactly 512.
All inputs are finite; a program needn't handle non-finite values.
Results may differ from the reference program's by a relative error of at most 0.0075.
Values may be sent and summed in bfloat16 or wider, within the bound.
A program may use at most 128 MiB of HBM per device.

```python
import math
import jax
import jax.numpy as jnp
import numpy as np
from jax import lax

HEAD_FEATURES = 64
STATE_ENTRIES = 256
LOCAL_HEADS = 128
SHARED_GROUPS = 8
BLOCK = 8
DOCUMENTS_PER_ROW = 4
BLK_DEV = 16
TOK_DEV = 128
CAP = 16
ROW_LENGTH = 1024
BLOCK_LENGTH = 128
N_DP = 2
N_PHASE = 4


def block_levels(key, shape, shards, low, largest):
    gain = 1.0
    for position, parts in shards:
        draws = jax.random.uniform(jax.random.fold_in(jax.random.fold_in(key, 6), position), (parts,), jnp.float32, low / len(shards), largest / len(shards))
        gain = gain * jnp.repeat(jnp.exp(draws), shape[position] // parts).reshape((-1,) + (1,) * (len(shape) - 1 - position))
    return gain


def split_up(count, total, most, slope):
    loads = [(1 << 20) // math.isqrt(grade ** slope) + 1 for grade in range(2, count + 1)]
    rest, given = total - most - (count - 1), [1] * (count - 1)
    while rest > 0:
        candidates = [i for i in range(count - 1) if given[i] < most]
        pool, budget = sum([loads[i] for i in candidates]), rest
        for i in candidates:
            extra = min(most - given[i], max(1, budget * loads[i] // pool), rest)
            given[i] = given[i] + extra
            rest = rest - extra
    return np.array([most] + given)


def ragged_sizes(key, number_of, total, reach, lean):
    if number_of == 2:
        one = jax.random.randint(key, (), max(1, total - reach), min(reach, total - 1) + 1)
        return jnp.stack([one, total - one])
    sizes = jnp.asarray(split_up(number_of, total, reach, lean), jnp.int32)
    couples = (number_of - 1) // 2
    donor, sink = sizes[1:1 + 2 * couples:2], sizes[2:2 + 2 * couples:2]
    room = jnp.minimum(donor - 1, reach - sink)
    shifted = jax.random.randint(jax.random.fold_in(key, 1), (couples,), 0, 1 << 20) % (room + 1)
    sizes = sizes.at[1:1 + 2 * couples:2].set(donor - shifted).at[2:2 + 2 * couples:2].set(sink + shifted)
    return sizes[jax.random.permutation(jax.random.fold_in(key, 2), number_of)]


def shared_out(own_key, own, number, rows, number_of, top, most, lean):
    sequence = jax.random.permutation(own_key, number_of)
    heavy_load, ordinary = shares(number_of, rows * top, most, lean, True), shares(number_of, rows * top, most, lean, False)
    places = jnp.arange(number_of)

    def named(sizes, offset_by):
        used = int((sizes > 0).sum())
        fixed = max(1, used // 4)
        shifted = fixed + (places - fixed + offset_by * (used - fixed)) % max(1, number_of - fixed)
        return jnp.zeros((number_of,), jnp.int32).at[sequence[jnp.where(places < fixed, places, shifted)]].set(jnp.asarray(sizes, jnp.int32))

    sizes = jnp.where(number % 4 == 0, named(heavy_load, number // 4), named(ordinary, number - number // 4 - 1))
    mixed = jax.random.permutation(jax.random.fold_in(own, 3), number_of)
    giver, taker = mixed[0:number_of // 2 * 2:2], mixed[1:number_of // 2 * 2:2]
    room = jnp.minimum(sizes[giver] - 1, most - sizes[taker]) // 2
    room = jnp.where((giver == sequence[0]) | (taker == sequence[0]) | (sizes[taker] == 0), 0, jnp.maximum(room, 0))
    shifted = jax.random.randint(jax.random.fold_in(own, 4), (number_of // 2,), 0, 1 << 20) % (room + 1)
    sizes = sizes.at[giver].add(-shifted).at[taker].add(shifted)
    labels = jnp.searchsorted(jnp.cumsum(sizes), jnp.arange(rows * top), side="right").astype(jnp.int32)
    table = labels.reshape(top, rows).T
    table = table[jax.random.permutation(jax.random.fold_in(own, 1), rows)]
    offset_by = jax.random.randint(jax.random.fold_in(own, 2), (rows, 1), 0, top)
    return jnp.take_along_axis(table, (jnp.arange(top)[None, :] + offset_by) % top, axis=1)


def shares(number_of, total, bound, slope, full):
    loads = [(1 << 20) // math.isqrt(rank ** slope) + 1 for rank in range(1, number_of + 1)]
    largest = bound if full else min(bound, max(-(-total // number_of), total * loads[0] // sum(loads)))
    least = 1 if total - largest >= number_of - 1 else 0
    given, spare = [largest] + [least] * (number_of - 1), total - largest - least * (number_of - 1)
    while spare > 0:
        free = [i for i in range(1, number_of) if given[i] < largest] or [i for i in range(1, number_of) if given[i] < bound]
        pool, budget = sum([loads[i] for i in free]), spare
        for i in free:
            addition = min(bound - given[i], max(1, budget * loads[i] // pool), spare)
            given[i] = given[i] + addition
            spare = spare - addition
    return np.array(given)


def gaussian(rng, dims, width, reach, cuts=(), held_as=jnp.bfloat16):
    loudness = block_levels(rng, dims, cuts, -0.22, 0.18) if cuts else 1.0
    drawn = jax.random.normal(rng, dims, jnp.float32) * width * loudness
    return jnp.minimum(jnp.maximum(drawn, -reach), reach).astype(held_as)


def setup_inputs(seed: int = 0) -> dict:
    splits = jax.random.split(jax.random.key(seed), 9)
    tokens = gaussian(splits[0], (N_DP, N_PHASE * TOK_DEV, LOCAL_HEADS * HEAD_FEATURES), 1.0, 6.0, ((0, 2), (1, 4), (2, 4)))
    bc_proj = gaussian(splits[1], (N_DP, N_PHASE * TOK_DEV, 2, SHARED_GROUPS * STATE_ENTRIES), 0.0625, 0.3984375, ((0, 2), (1, 4), (3, 4)))
    step_sizes = jnp.clip(jnp.exp(math.log(2.0) - 1.3862944 * jax.random.uniform(splits[2], (N_DP, N_PHASE * BLK_DEV, LOCAL_HEADS * BLOCK), jnp.float32) ** block_levels(splits[2], (N_DP, N_PHASE * BLK_DEV, LOCAL_HEADS * BLOCK), ((0, 2), (1, 4), (2, 4)), -0.2, 0.2)), 0.5, 2.0).astype(jnp.bfloat16)
    decay_rates = jnp.clip(jnp.exp(math.log(0.02) - 4.405743 * jax.random.uniform(splits[3], (LOCAL_HEADS,), jnp.float32) ** block_levels(splits[3], (LOCAL_HEADS,), ((0, 4),), -0.2, 0.2)), 0.00024414062, 0.02)
    direct_weight = jnp.clip(0.5 + 1.0 * jax.random.uniform(splits[4], (LOCAL_HEADS,), jnp.float32) ** block_levels(splits[4], (LOCAL_HEADS,), ((0, 4),), -0.2, 0.2), 0.5, 1.5)
    norm_gain = jnp.clip(1.0 + 0.18 * jax.random.normal(splits[5], (LOCAL_HEADS * HEAD_FEATURES,), jnp.float32), 0.1, 1.9)
    routes_keys = jax.random.split(jax.random.fold_in(splits[6], 1), N_DP * (N_PHASE * BLK_DEV) // BLK_DEV)
    routes_turns = jax.random.permutation(jax.random.fold_in(splits[6], 3), N_DP * (N_PHASE * BLK_DEV) // BLK_DEV)
    routes = jax.vmap(lambda own, number: shared_out(jax.random.fold_in(splits[6], 2), own, number, BLK_DEV, N_DP, 1, CAP, 2))(routes_keys, routes_turns).reshape((N_DP, N_PHASE * BLK_DEV, 1))
    segments = jax.vmap(lambda own: jnp.searchsorted(jnp.cumsum(ragged_sizes(own, DOCUMENTS_PER_ROW, ROW_LENGTH, ROW_LENGTH // 2, 0)), jnp.arange(ROW_LENGTH), side="right"))(jax.random.split(splits[7], N_DP)).reshape((N_DP, ROW_LENGTH)).astype(jnp.int32)
    return dict(tokens=tokens, bc_proj=bc_proj, step_sizes=step_sizes, decay_rates=decay_rates, direct_weight=direct_weight, norm_gain=norm_gain, routes=routes, segments=segments)


EPSILON = 1e-05
PRECISE = lax.Precision.HIGHEST

def stretch_pass(carry_state, prior_id, x_stretch, b_stretch, c_stretch, dt_stretch, doc_ids, decay_rates):
    span_len = x_stretch.shape[0]
    head_count = x_stretch.shape[1]
    groups = b_stretch.shape[1]
    per_group = head_count // groups
    log_decay = jnp.cumsum(-decay_rates[:, None] * dt_stretch, axis=1)
    positions = jnp.arange(span_len)
    same_doc = (doc_ids[:, None] == doc_ids[None, :]) & (positions[:, None] >= positions[None, :])
    gaps = jnp.minimum(log_decay[:, :, None] - log_decay[:, None, :], 0.0)
    decay_mat = jnp.where(same_doc[None], jnp.exp(gaps), 0.0) * dt_stretch[:, None, :]
    scores = jnp.einsum('ign,jgn->gij', c_stretch, b_stretch, precision=PRECISE)
    weights = decay_mat.reshape(groups, per_group, span_len, span_len) * scores[:, None]
    x_groups = x_stretch.reshape(span_len, groups, per_group, -1)
    inside = jnp.einsum('gkij,jgkp->igkp', weights, x_groups, precision=PRECISE)
    state_groups = carry_state.reshape(groups, per_group, carry_state.shape[1], carry_state.shape[2])
    carried = jnp.einsum('ign,gkpn->igkp', c_stretch, state_groups, precision=PRECISE)
    keep_in = jnp.where(doc_ids[None, :] == prior_id, jnp.exp(log_decay), 0.0)
    result = inside + keep_in.T.reshape(span_len, groups, per_group)[..., None] * carried
    last_id = doc_ids[-1]
    tail_decay = jnp.where(doc_ids[None, :] == last_id, jnp.exp(log_decay[:, -1:] - log_decay), 0.0) * dt_stretch
    scaled = x_groups * tail_decay.T.reshape(span_len, groups, per_group)[..., None]
    update = jnp.einsum('jgkp,jgn->gkpn', scaled, b_stretch, precision=PRECISE).reshape(carry_state.shape)
    through = jnp.where(prior_id == last_id, jnp.exp(log_decay[:, -1]), 0.0)
    new_state = through[:, None, None] * carry_state + update
    return (new_state, last_id, result.reshape(span_len, head_count, -1))

def row_pass(input_row, b_row, c_row, dt_row, doc_row, decay_rates, direct_weight):
    block_count = ROW_LENGTH // BLOCK_LENGTH
    input_single = input_row.astype(jnp.float32).reshape(ROW_LENGTH, LOCAL_HEADS, HEAD_FEATURES)
    x_stretches = input_single.reshape(block_count, BLOCK_LENGTH, LOCAL_HEADS, HEAD_FEATURES)
    b_stretches = b_row.astype(jnp.float32).reshape(block_count, BLOCK_LENGTH, SHARED_GROUPS, STATE_ENTRIES)
    c_stretches = c_row.astype(jnp.float32).reshape(block_count, BLOCK_LENGTH, SHARED_GROUPS, STATE_ENTRIES)
    dt_stretches = dt_row.reshape(LOCAL_HEADS, block_count, BLOCK_LENGTH).transpose(1, 0, 2)
    doc_stretches = doc_row.reshape(block_count, BLOCK_LENGTH)

    def advance(carry, pieces):
        new_state, last_id, result = stretch_pass(carry[0], carry[1], pieces[0], pieces[1], pieces[2], pieces[3], pieces[4], decay_rates)
        return ((new_state, last_id), result)
    start_carry = (jnp.zeros((LOCAL_HEADS, HEAD_FEATURES, STATE_ENTRIES), jnp.float32), jnp.array(-1.0, jnp.float32))
    _, scan_results = lax.scan(advance, start_carry, (x_stretches, b_stretches, c_stretches, dt_stretches, doc_stretches))
    output_row = scan_results.reshape(ROW_LENGTH, LOCAL_HEADS, HEAD_FEATURES) + direct_weight[None, :, None] * input_single
    return output_row.astype(jnp.bfloat16).reshape(ROW_LENGTH, LOCAL_HEADS * HEAD_FEATURES)

def reference(tokens, bc_proj, step_sizes, decay_rates, direct_weight, norm_gain, routes, segments):
    feature_width = LOCAL_HEADS * HEAD_FEATURES
    targets = routes[:, :, 0].reshape(N_DP, N_PHASE, BLK_DEV).astype(jnp.int32)
    positions = jnp.arange(BLK_DEV)
    earlier = positions[:, None] > positions[None, :]
    slot_rank = lax.optimization_barrier(jnp.sum((targets[..., :, None] == targets[..., None, :]) & earlier, axis=-1)).astype(jnp.int32)
    source_ids = jnp.arange(N_DP).astype(jnp.int32)[:, None, None]
    phase_ids = jnp.arange(N_PHASE).astype(jnp.int32)[None, :, None]
    x_blocks = tokens.reshape(N_DP, N_PHASE, BLK_DEV, BLOCK, feature_width)
    input_rows = jnp.zeros((N_DP, N_PHASE, N_DP, CAP, BLOCK, feature_width), jnp.bfloat16).at[targets, phase_ids, source_ids, slot_rank].set(x_blocks)
    bc_blocks = bc_proj.reshape(N_DP, N_PHASE, BLK_DEV, BLOCK, 2, SHARED_GROUPS, STATE_ENTRIES)
    input_output_rows = jnp.zeros((N_DP, N_PHASE, N_DP, CAP, BLOCK, 2, SHARED_GROUPS, STATE_ENTRIES), jnp.bfloat16).at[targets, phase_ids, source_ids, slot_rank].set(bc_blocks)
    dt_blocks = step_sizes.reshape(N_DP, N_PHASE, BLK_DEV, LOCAL_HEADS, BLOCK)
    step_size_rows = jnp.zeros((N_DP, N_PHASE, N_DP, CAP, LOCAL_HEADS, BLOCK), jnp.bfloat16).at[targets, phase_ids, source_ids, slot_rank].set(dt_blocks)
    input_rows = input_rows.reshape(N_DP, ROW_LENGTH, feature_width)
    input_proj_rows = input_output_rows[:, :, :, :, :, 0].reshape(N_DP, ROW_LENGTH, SHARED_GROUPS, STATE_ENTRIES)
    output_proj_rows = input_output_rows[:, :, :, :, :, 1].reshape(N_DP, ROW_LENGTH, SHARED_GROUPS, STATE_ENTRIES)
    step_size_rows = step_size_rows.transpose(0, 4, 1, 2, 3, 5).reshape(N_DP, LOCAL_HEADS, ROW_LENGTH).astype(jnp.float32)
    doc_rows = segments.astype(jnp.float32)

    def one_row(pieces):
        return row_pass(pieces[0], pieces[1], pieces[2], pieces[3], pieces[4], decay_rates, direct_weight)
    y_rows = lax.map(one_row, (input_rows, input_proj_rows, output_proj_rows, step_size_rows, doc_rows))
    y_slots = y_rows.reshape(N_DP, N_PHASE, N_DP, CAP, BLOCK, feature_width)
    moved = y_slots[targets, phase_ids, source_ids, slot_rank]
    moved = moved.reshape(N_DP, N_PHASE * BLK_DEV * BLOCK, feature_width).astype(jnp.float32)
    square_sums = lax.optimization_barrier(jnp.sum(moved * moved, axis=-1, keepdims=True))
    mixed = moved * lax.rsqrt(square_sums / feature_width + EPSILON) * norm_gain
    return mixed.astype(jnp.bfloat16)
```

```python
import functools

import jax
import jax.numpy as jnp
from jax import lax
from jax.experimental import pallas as pl
from jax.experimental.pallas import tpu as pltpu
from jax.sharding import PartitionSpec as P

HEAD_FEATURES = 64
STATE_ENTRIES = 256
BLOCK = 8
EPSILON = 1e-05
LANES = 128
ROW_KEY = 1024.0
MESH = pl.DeviceIdType.MESH


def kernel(
    n_phase, n_tensor, total_features,
    x_ref, bc_ref, dt_ref, decay_ref, direct_ref, gain_ref, meta_ref,
    out_ref,
    xall, bcall, dtall, meta, metaprev, local, inside, hin, hout, ysend, ymine, sums, mysum,
    s_meta, r_meta, s_dt, r_dt, s_bc, r_bc, s_x, r_x, s_h, r_h, s_y, r_y, s_sum, r_sum,
):
    f32, bf16 = jnp.float32, jnp.bfloat16
    me, phase, place = lax.axis_index("dp"), lax.axis_index("phase"), lax.axis_index("tensor")
    other = 1 - me
    tok, width = x_ref.shape
    half = width // 2
    chunks = half // LANES
    n = STATE_ENTRIES
    partner = (other, phase, place)
    first, last = phase == 0, phase == n_phase - 1

    barrier = pltpu.get_barrier_semaphore()
    pl.semaphore_signal(barrier, inc=1, device_id=partner, device_id_type=MESH)
    for k in range(1, n_tensor):
        pl.semaphore_signal(
            barrier, inc=1, device_id=(me, phase, lax.rem(place + k, n_tensor)), device_id_type=MESH
        )

    @pl.when(phase > 0)
    def _():
        for d in (me, other):
            pl.semaphore_signal(barrier, inc=1, device_id=(d, phase - 1, place), device_id_type=MESH)

    @pl.when(phase < n_phase - 1)
    def _():
        for d in (me, other):
            pl.semaphore_signal(barrier, inc=1, device_id=(d, phase + 1, place), device_id_type=MESH)

    peers = n_tensor + 2 * jnp.minimum(phase, 1) + 2 * jnp.minimum(n_phase - 1 - phase, 1)
    pl.semaphore_wait(barrier, peers)

    def remote(src, dst, send, recv, device):
        return pltpu.make_async_remote_copy(
            src_ref=src, dst_ref=dst, send_sem=send, recv_sem=recv,
            device_id=device, device_id_type=MESH,
        )

    my_rows = pl.ds(pl.multiple_of(me * tok, tok), tok)
    other_rows = pl.ds(pl.multiple_of(other * tok, tok), tok)
    my_group = pl.ds(pl.multiple_of(me * n, n), n)
    other_group = pl.ds(pl.multiple_of(other * n, n), n)
    my_c = pl.ds(pl.multiple_of(2 * n + me * n, n), n)
    other_c = pl.ds(pl.multiple_of(2 * n + other * n, n), n)

    copies = [
        remote(meta_ref, meta.at[me], s_meta.at[0], r_meta.at[0], partner),
        remote(dt_ref.at[other], dtall.at[my_rows], s_dt, r_dt, partner),
        remote(bc_ref.at[:, other_group], bcall.at[my_rows, pl.ds(0, n)], s_bc.at[0], r_bc.at[0], partner),
        remote(bc_ref.at[:, other_c], bcall.at[my_rows, pl.ds(n, n)], s_bc.at[1], r_bc.at[1], partner),
    ]
    x_copies = [
        remote(
            x_ref.at[:, pl.ds(pl.multiple_of(other * half + c * LANES, LANES), LANES)],
            xall.at[my_rows, pl.ds(c * LANES, LANES)],
            s_x.at[c], r_x.at[c], partner,
        )
        for c in range(chunks)
    ]
    after = jnp.minimum(phase + 1, n_phase - 1)
    ahead = [
        remote(meta_ref, metaprev.at[me], s_meta.at[1 + i], r_meta.at[1 + i], (d, after, place))
        for i, d in enumerate((me, other))
    ]
    h_copies = [
        remote(hout.at[c], hin.at[c], s_h.at[c], r_h.at[c], (me, after, place)) for c in range(chunks)
    ]
    for copy in copies[:2]:
        copy.start()

    @pl.when(phase < n_phase - 1)
    def _():
        for copy in ahead:
            copy.start()

    for copy in copies[2:] + x_copies:
        copy.start()

    meta[me] = meta_ref[...]
    dtall[my_rows] = dt_ref[me]
    bcall[my_rows, pl.ds(0, n)] = bc_ref[:, my_group]
    bcall[my_rows, pl.ds(n, n)] = bc_ref[:, my_c]
    xall[my_rows, :] = x_ref[:, pl.ds(pl.multiple_of(me * half, half), half)]

    @pl.when(first)
    def _():
        metaprev[...] = jnp.full_like(metaprev, -(2.0**20))
        hin[...] = jnp.zeros_like(hin)

    copies[0].wait_recv()

    @pl.when(phase > 0)
    def _():
        for copy in ahead:
            copy.wait_recv()

    slots = lax.broadcasted_iota(jnp.int32, (tok, tok), 0).astype(f32)
    row_lanes, key_lanes, row_subl, key_subl = [], [], [], []
    for j in range(2):
        rows = meta[j, 0:1, :]
        places = jnp.where(slots == meta[j, 1:2, :], 1.0, 0.0).astype(bf16)
        found = [
            jnp.dot(meta[d].astype(bf16), places, preferred_element_type=f32)[2 + j : 3 + j, :]
            for d in range(2)
        ]
        key = rows * ROW_KEY + jnp.where(rows == 0.0, found[0], found[1])
        row_lanes.append(rows)
        key_lanes.append(key)
        row_subl.append(jnp.broadcast_to(rows, (tok, tok)).T)
        key_subl.append(jnp.broadcast_to(key, (tok, tok)).T)
    row_lane, key_lane = jnp.concatenate(row_lanes, 1), jnp.concatenate(key_lanes, 1)
    row_sub, key_sub = jnp.concatenate(row_subl, 0), jnp.concatenate(key_subl, 0)
    both = 2 * tok
    causal = lax.broadcasted_iota(jnp.int32, (both, both), 0) >= lax.broadcasted_iota(
        jnp.int32, (both, both), 1
    )
    row_sub2 = jnp.concatenate([row_sub, row_sub], 1)
    key_sub2 = jnp.concatenate([key_sub, key_sub], 1)
    same_row = jnp.where(causal & (row_sub2 == row_lane), 1.0, 0.0).astype(bf16)
    same_doc = jnp.where(causal & (key_sub2 == key_lane), 1.0, 0.0)

    ends = [meta[d, 3:4, tok - 1 : tok] for d in range(2)]
    befores = [metaprev[d, 3:4, tok - 1 : tok] for d in range(2)]
    through = [jnp.where(ends[d] == befores[d], 1.0, 0.0) for d in range(2)]

    copies[1].wait_recv()
    decay = decay_ref[me, 0:1, :]
    dt = dtall[...]
    log_decay = -decay * jnp.dot(same_row, dt, preferred_element_type=f32)
    grow = jnp.exp(-log_decay) * dt.astype(f32)
    shrink = jnp.exp(log_decay)
    picks = jnp.where(
        lax.broadcasted_iota(jnp.int32, (16, both), 0).astype(f32) == row_lane, 1.0, 0.0
    ).astype(bf16)
    whole = jnp.exp(-decay * jnp.dot(picks, dt, preferred_element_type=f32))

    copies[2].wait_recv()
    b_mat = bcall[:, 0:n]
    b_float = b_mat.astype(f32)
    b_both_t = jnp.concatenate(
        [
            jnp.where(key_sub2 == ends[d] + d * ROW_KEY, b_float, 0.0).T.astype(bf16)
            for d in range(2)
        ],
        0,
    )
    copies[3].wait_recv()
    c_mat = bcall[:, n : 2 * n]
    c_float = c_mat.astype(f32)
    c_both = jnp.concatenate(
        [
            jnp.where(key_sub2 == befores[d] + d * ROW_KEY, c_float, 0.0).astype(bf16)
            for d in range(2)
        ],
        1,
    )
    scores = lax.dot_general(c_mat, b_mat, (((1,), (1,)), ((), ())), preferred_element_type=f32)
    scores = (scores * same_doc).astype(bf16)

    def spread(a, c):
        low = lax.broadcasted_iota(jnp.int32, (a.shape[0], LANES), 1) < HEAD_FEATURES
        shape = (a.shape[0], LANES)
        return jnp.where(
            low,
            jnp.broadcast_to(a[:, 2 * c : 2 * c + 1], shape),
            jnp.broadcast_to(a[:, 2 * c + 1 : 2 * c + 2], shape),
        )

    for c in range(chunks):
        x_copies[c].wait_recv()
        cols = pl.ds(c * LANES, LANES)
        scaled = (xall[:, cols].astype(f32) * spread(grow, c)).astype(bf16)
        keep = spread(whole, c)
        update = jnp.dot(b_both_t, scaled, preferred_element_type=f32)
        for d in range(2):
            local[c, d * n : (d + 1) * n, :] = update[d * n : (d + 1) * n] * keep[d : d + 1]

        @pl.when(first)
        def _():
            hout[c] = local[c].astype(bf16)
            h_copies[c].start()

        inside[:, cols] = jnp.dot(scores, scaled, preferred_element_type=f32)

    squares = jnp.zeros((tok, LANES), f32)
    y_copies = []
    for c in range(chunks):
        cols = pl.ds(c * LANES, LANES)

        @pl.when(phase > 0)
        def _():
            h_copies[c].wait_recv()

        @pl.when((phase > 0) & (phase < n_phase - 1))
        def _():
            keep = spread(whole, c)
            for d in range(2):
                rows = slice(d * n, (d + 1) * n)
                hout[c, rows, :] = (
                    local[c, rows, :] + (keep[d : d + 1] * through[d]) * hin[c, rows, :].astype(f32)
                ).astype(bf16)
            h_copies[c].start()

        carried = jnp.dot(c_both, hin[c], preferred_element_type=f32)
        y = spread(shrink, c) * (inside[:, cols] + carried) + direct_ref[
            me, 0:1, c * LANES : (c + 1) * LANES
        ] * xall[:, cols].astype(f32)
        ysend[c] = y.astype(bf16)
        here = pl.ds(pl.multiple_of(me * half + c * LANES, LANES), LANES)
        copy = remote(ysend.at[c, other_rows], ymine.at[:, here], s_y.at[c], r_y.at[c], partner)
        copy.start()
        y_copies.append(copy)
        own = ysend[c, my_rows]
        ymine[:, here] = own
        own = own.astype(f32)
        squares = squares + own * own

    for c in range(chunks):
        y_copies[c].wait_recv()
        there = pl.ds(pl.multiple_of(other * half + c * LANES, LANES), LANES)
        got = ymine[:, there].astype(f32)
        squares = squares + got * got

    per_token = jnp.broadcast_to(jnp.sum(squares, axis=1, keepdims=True), (tok, tok)).T[0:8, :]
    mysum[...] = per_token
    sum_copies = []
    for k in range(1, n_tensor):
        copy = remote(
            mysum, sums.at[k - 1], s_sum.at[k - 1], r_sum.at[k - 1],
            (me, phase, lax.rem(place + k, n_tensor)),
        )
        copy.start()
        sum_copies.append(copy)
    total = per_token
    for k in range(1, n_tensor):
        sum_copies[k - 1].wait_recv()
        total = total + sums[k - 1]
    scale = lax.rsqrt(total[0:1, :] / total_features + EPSILON)
    scale = jnp.broadcast_to(scale, (tok, tok)).T
    for c in range(2 * chunks):
        cols = pl.ds(c * LANES, LANES)
        out_ref[:, cols] = (ymine[:, cols].astype(f32) * scale * gain_ref[0:1, cols]).astype(bf16)

    for copy in copies + x_copies + y_copies + sum_copies:
        copy.wait_send()

    @pl.when(phase < n_phase - 1)
    def _():
        for copy in ahead + h_copies:
            copy.wait_send()


def per_device(
    n_phase, n_tensor,
    tokens, bc_proj, step_sizes, decay_rates, direct_weight, norm_gain, routes, segments,
):
    tok, width = tokens.shape[1:]
    heads = decay_rates.shape[0]
    blocks = tok // BLOCK
    half = width // 2
    chunks = half // LANES
    n = STATE_ENTRIES
    f32, bf16 = jnp.float32, jnp.bfloat16

    targets = routes[0, :, 0]
    order = jnp.arange(blocks)
    earlier = order[:, None] > order[None, :]
    rank = jnp.sum((targets[:, None] == targets[None, :]) & earlier, axis=1)
    row = jnp.broadcast_to(targets[:, None], (blocks, BLOCK)).reshape(1, tok)
    slot = (rank[:, None] * BLOCK + jnp.arange(BLOCK)[None, :]).reshape(1, tok)
    meta = jnp.concatenate(
        [row, slot, segments.reshape(2, tok), jnp.zeros((4, tok), jnp.int32)], 0
    ).astype(f32)
    dt = step_sizes.reshape(blocks, 2, heads // 2, BLOCK).transpose(1, 0, 3, 2)
    dt = dt.reshape(2, tok, heads // 2)
    dt = jnp.pad(dt, ((0, 0), (0, 0), (0, LANES - heads // 2)))
    decay = jnp.pad(decay_rates.reshape(2, 1, heads // 2), ((0, 0), (0, 7), (0, LANES - heads // 2)))
    direct = jnp.broadcast_to(
        jnp.repeat(direct_weight, HEAD_FEATURES).reshape(2, 1, half), (2, 8, half)
    )
    dma = pltpu.SemaphoreType.DMA
    vmem = pltpu.VMEM
    out = pl.pallas_call(
        functools.partial(kernel, n_phase, n_tensor, float(n_tensor * width)),
        out_shape=jax.ShapeDtypeStruct((tok, width), bf16),
        in_specs=[pl.BlockSpec(memory_space=pltpu.VMEM)] * 7,
        out_specs=pl.BlockSpec(memory_space=pltpu.VMEM),
        scratch_shapes=[
            vmem((2 * tok, half), bf16),
            vmem((2 * tok, 2 * n), bf16),
            vmem((2 * tok, LANES), bf16),
            vmem((2, 8, tok), f32),
            vmem((2, 8, tok), f32),
            vmem((chunks, 2 * n, LANES), f32),
            vmem((2 * tok, half), f32),
            vmem((chunks, 2 * n, LANES), bf16),
            vmem((chunks, 2 * n, LANES), bf16),
            vmem((chunks, 2 * tok, LANES), bf16),
            vmem((tok, width), bf16),
            vmem((n_tensor - 1, 8, tok), f32),
            vmem((8, tok), f32),
            dma((3,)), dma((3,)), dma, dma, dma((2,)), dma((2,)),
            dma((chunks,)), dma((chunks,)), dma((chunks,)), dma((chunks,)),
            dma((chunks,)), dma((chunks,)), dma((n_tensor - 1,)), dma((n_tensor - 1,)),
        ],
        compiler_params=pltpu.CompilerParams(
            collective_id=0, has_side_effects=True, vmem_limit_bytes=40 * 2**20
        ),
    )(
        tokens.reshape(tok, width), bc_proj.reshape(tok, -1), dt, decay, direct,
        norm_gain.reshape(1, width), meta,
    )
    return out.reshape(1, tok, width)


def solution(mesh):
    return jax.shard_map(
        functools.partial(per_device, mesh.shape["phase"], mesh.shape["tensor"]),
        mesh=mesh,
        in_specs=(
            P("dp", "phase", "tensor"),
            P("dp", "phase", None, "tensor"),
            P("dp", "phase", "tensor"),
            P("tensor"),
            P("tensor"),
            P("tensor"),
            P("dp", "phase", None),
            P("dp", "phase"),
        ),
        out_specs=P("dp", "phase", "tensor"),
        check_vma=False,
    )
```

```python
import functools

import jax
import jax.numpy as jnp
from jax import lax
from jax.experimental import pallas as pl
from jax.experimental.pallas import tpu as pltpu
from jax.sharding import PartitionSpec as P

HEAD_FEATURES = 64
STATE_ENTRIES = 256
BLOCK = 8
EPSILON = 1e-05
LANES = 128
ROW_KEY = 1024.0
MESH = pl.DeviceIdType.MESH


def kernel(
    n_phase, n_tensor, total_features,
    x_ref, bc_ref, dt_ref, head_ref, meta_ref,
    y_ref, scale_ref,
    xall, bcall, dtall, meta, metaprev, local, xscaled, hin, hout, ysend, ymine, sums, mysum,
    s_meta, r_meta, s_dt, r_dt, s_bc, r_bc, s_x, r_x, s_h, r_h, s_y, r_y, s_sum, r_sum, s_own,
):
    f32, bf16 = jnp.float32, jnp.bfloat16
    me, phase, place = lax.axis_index("dp"), lax.axis_index("phase"), lax.axis_index("tensor")
    other = 1 - me
    tok, width = x_ref.shape
    half = width // 2
    chunks = half // LANES
    n = STATE_ENTRIES
    heads = dt_ref.shape[1]
    partner = (other, phase, place)
    first = phase == 0

    my_rows = pl.ds(pl.multiple_of(me * tok, tok), tok)
    other_rows = pl.ds(pl.multiple_of(other * tok, tok), tok)
    my_group = pl.ds(pl.multiple_of(me * n, n), n)
    other_group = pl.ds(pl.multiple_of(other * n, n), n)
    my_c = pl.ds(pl.multiple_of(2 * n + me * n, n), n)
    other_c = pl.ds(pl.multiple_of(2 * n + other * n, n), n)
    own_x = pltpu.make_async_copy(
        x_ref.at[:, pl.ds(pl.multiple_of(me * half, half), half)], xall.at[my_rows], s_own
    )
    own_x.start()

    barrier = pltpu.get_barrier_semaphore()
    pl.semaphore_signal(barrier, inc=1, device_id=partner, device_id_type=MESH)
    for k in range(1, n_tensor):
        pl.semaphore_signal(
            barrier, inc=1, device_id=(me, phase, lax.rem(place + k, n_tensor)), device_id_type=MESH
        )

    @pl.when(phase > 0)
    def _():
        for d in (me, other):
            pl.semaphore_signal(barrier, inc=1, device_id=(d, phase - 1, place), device_id_type=MESH)

    @pl.when(phase < n_phase - 1)
    def _():
        for d in (me, other):
            pl.semaphore_signal(barrier, inc=1, device_id=(d, phase + 1, place), device_id_type=MESH)

    peers = n_tensor + 2 * jnp.minimum(phase, 1) + 2 * jnp.minimum(n_phase - 1 - phase, 1)
    pl.semaphore_wait(barrier, peers)

    def remote(src, dst, send, recv, device):
        return pltpu.make_async_remote_copy(
            src_ref=src, dst_ref=dst, send_sem=send, recv_sem=recv,
            device_id=device, device_id_type=MESH,
        )

    copies = [
        remote(meta_ref, meta.at[me], s_meta.at[0], r_meta.at[0], partner),
        remote(dt_ref.at[other], dtall.at[me], s_dt, r_dt, partner),
        remote(bc_ref.at[:, other_group], bcall.at[my_rows, pl.ds(0, n)], s_bc.at[0], r_bc.at[0], partner),
        remote(bc_ref.at[:, other_c], bcall.at[my_rows, pl.ds(n, n)], s_bc.at[1], r_bc.at[1], partner),
    ]
    x_copies = [
        remote(
            x_ref.at[:, pl.ds(pl.multiple_of(other * half + c * LANES, LANES), LANES)],
            xall.at[my_rows, pl.ds(c * LANES, LANES)],
            s_x.at[c], r_x.at[c], partner,
        )
        for c in range(chunks)
    ]
    after = jnp.minimum(phase + 1, n_phase - 1)
    ahead = [
        remote(meta_ref, metaprev.at[me], s_meta.at[1 + i], r_meta.at[1 + i], (d, after, place))
        for i, d in enumerate((me, other))
    ]
    h_copies = [
        [
            remote(
                hout.at[c, pl.ds(d * n, n)], hin.at[c, pl.ds(d * n, n)],
                s_h.at[2 * c + d], r_h.at[2 * c + d], (me, after, place),
            )
            for d in range(2)
        ]
        for c in range(chunks)
    ]
    for copy in copies[:3] + x_copies[:4] + copies[3:] + x_copies[4:]:
        copy.start()

    @pl.when(phase < n_phase - 1)
    def _():
        for copy in ahead:
            copy.start()

    meta[me] = meta_ref[...]
    dtall[me] = dt_ref[me]
    bcall[my_rows, pl.ds(0, n)] = bc_ref[:, my_group]
    bcall[my_rows, pl.ds(n, n)] = bc_ref[:, my_c]

    @pl.when(first)
    def _():
        metaprev[...] = jnp.full_like(metaprev, -(2.0**20))
        hin[...] = jnp.zeros_like(hin)

    both = 2 * tok
    at_row = lax.broadcasted_iota(jnp.int32, (both, both), 0)
    at_col = lax.broadcasted_iota(jnp.int32, (both, both), 1)
    causal = at_row >= at_col
    unit = jnp.where(at_row == at_col, 1.0, 0.0).astype(bf16)
    slots = lax.broadcasted_iota(jnp.int32, (tok, tok), 0).astype(f32)

    copies[0].wait_recv()

    row_lanes, key_lanes, row_subl, key_subl = [], [], [], []
    for j in range(2):
        rows = meta[j, 0:1, :]
        places = jnp.where(slots == meta[j, 1:2, :], 1.0, 0.0).astype(bf16)
        found = [
            jnp.dot(meta[d].astype(bf16), places, preferred_element_type=f32)[2 + j : 3 + j, :]
            for d in range(2)
        ]
        key = rows * ROW_KEY + jnp.where(rows == 0.0, found[0], found[1])
        row_lanes.append(rows)
        key_lanes.append(key)
        row_subl.append(jnp.broadcast_to(rows, (tok, tok)).T)
        key_subl.append(jnp.broadcast_to(key, (tok, tok)).T)
    row_lane, key_lane = jnp.concatenate(row_lanes, 1), jnp.concatenate(key_lanes, 1)
    row_sub, key_sub = jnp.concatenate(row_subl, 0), jnp.concatenate(key_subl, 0)
    row_sub2 = jnp.concatenate([row_sub, row_sub], 1)
    key_sub2 = jnp.concatenate([key_sub, key_sub], 1)
    same_row = jnp.where(causal & (row_sub2 == row_lane), 1.0, 0.0).astype(bf16)
    picks = jnp.where(
        lax.broadcasted_iota(jnp.int32, (16, both), 0).astype(f32) == row_lane, 1.0, 0.0
    ).astype(bf16)
    ends = [meta[d, 3:4, tok - 1 : tok] for d in range(2)]

    copies[1].wait_recv()
    decay = head_ref[me, 0:1, 0:heads]
    dt_lanes = jnp.concatenate([dtall[0], dtall[1]], 1)
    steps = lax.dot_general(
        jnp.concatenate([same_row, unit, picks], 0), dt_lanes,
        (((1,), (1,)), ((), ())), preferred_element_type=f32,
    )
    log_decay = -decay * steps[0:both]
    grow = jnp.exp(-log_decay) * steps[both : 2 * both]
    shrink = jnp.exp(log_decay)
    whole = jnp.exp(-decay * steps[2 * both : 2 * both + 8])

    copies[2].wait_recv()
    b_mat = bcall[:, 0:n]
    b_float = b_mat.astype(f32)
    b_both_t = jnp.concatenate(
        [
            jnp.where(key_sub2 == ends[d] + d * ROW_KEY, b_float, 0.0).T.astype(bf16)
            for d in range(2)
        ],
        0,
    )

    def spread(a, c):
        low = lax.broadcasted_iota(jnp.int32, (a.shape[0], LANES), 1) < HEAD_FEATURES
        shape = (a.shape[0], LANES)
        return jnp.where(
            low,
            jnp.broadcast_to(a[:, 2 * c : 2 * c + 1], shape),
            jnp.broadcast_to(a[:, 2 * c + 1 : 2 * c + 2], shape),
        )

    own_x.wait()
    for c in range(chunks):
        x_copies[c].wait_recv()
        cols = pl.ds(c * LANES, LANES)
        scaled = (xall[:, cols].astype(f32) * spread(grow, c)).astype(bf16)
        xscaled[:, cols] = scaled
        keep = spread(whole, c)
        update = jnp.dot(b_both_t, scaled, preferred_element_type=f32)
        update = jnp.concatenate(
            [update[d * n : (d + 1) * n] * keep[d : d + 1] for d in range(2)], 0
        )

        @pl.when(first)
        def _():
            hout[c] = update.astype(bf16)
            for d in range(2):
                h_copies[c][d].start()

        @pl.when(phase > 0)
        def _():
            local[c] = update

    @pl.when(phase > 0)
    def _():
        for copy in ahead:
            copy.wait_recv()

    befores = [metaprev[d, 3:4, tok - 1 : tok] for d in range(2)]
    through = [jnp.where(ends[d] == befores[d], 1.0, 0.0) for d in range(2)]
    copies[3].wait_recv()
    c_mat = bcall[:, n : 2 * n]
    c_float = c_mat.astype(f32)
    c_both = jnp.concatenate(
        [
            jnp.where(key_sub2 == befores[d] + d * ROW_KEY, c_float, 0.0).astype(bf16)
            for d in range(2)
        ],
        1,
    )
    scores = lax.dot_general(c_mat, b_mat, (((1,), (1,)), ((), ())), preferred_element_type=f32)
    scores = jnp.where(causal & (key_sub2 == key_lane), scores, 0.0).astype(bf16)

    squares = jnp.zeros((tok, LANES), f32)
    y_copies = []
    for c in range(chunks):
        cols = pl.ds(c * LANES, LANES)
        inside = jnp.dot(scores, xscaled[:, cols], preferred_element_type=f32)
        decayed = spread(shrink, c)
        direct = spread(head_ref[me, 1:2, :], c) * xall[:, cols].astype(f32)
        keep = spread(whole, c)
        for d in range(2):
            rows = pl.ds(d * n, n)

            @pl.when(phase > 0)
            def _():
                h_copies[c][d].wait_recv()

            @pl.when((phase > 0) & (phase < n_phase - 1))
            def _():
                hout[c, rows, :] = (
                    local[c, rows, :] + (keep[d : d + 1] * through[d]) * hin[c, rows, :].astype(f32)
                ).astype(bf16)
                h_copies[c][d].start()

        carried = jnp.dot(c_both, hin[c], preferred_element_type=f32)
        ysend[c] = (decayed * (inside + carried) + direct).astype(bf16)
        here = pl.ds(pl.multiple_of(me * half + c * LANES, LANES), LANES)
        copy = remote(ysend.at[c, other_rows], ymine.at[:, here], s_y.at[c], r_y.at[c], partner)
        copy.start()
        y_copies.append(copy)
        own = ysend[c, my_rows]
        y_ref[:, here] = own
        own = own.astype(f32)
        squares = squares + own * own

    for c in range(chunks):
        y_copies[c].wait_recv()
        there = pl.ds(pl.multiple_of(other * half + c * LANES, LANES), LANES)
        got = ymine[:, there]
        y_ref[:, there] = got
        got = got.astype(f32)
        squares = squares + got * got

    per_token = jnp.broadcast_to(jnp.sum(squares, axis=1, keepdims=True), (tok, tok)).T[0:8, :]
    mysum[...] = per_token
    sum_copies = []
    for k in range(1, n_tensor):
        copy = remote(
            mysum, sums.at[k - 1], s_sum.at[k - 1], r_sum.at[k - 1],
            (me, phase, lax.rem(place + k, n_tensor)),
        )
        copy.start()
        sum_copies.append(copy)
    total = per_token
    for copy in copies + x_copies + y_copies:
        copy.wait_send()

    @pl.when(phase < n_phase - 1)
    def _():
        for copy in ahead + [copy for pair in h_copies for copy in pair]:
            copy.wait_send()

    for k in range(1, n_tensor):
        sum_copies[k - 1].wait_recv()
        total = total + sums[k - 1]
    scale_ref[...] = lax.rsqrt(total / total_features + EPSILON)
    for copy in sum_copies:
        copy.wait_send()


def per_device(
    n_phase, n_tensor,
    tokens, bc_proj, step_sizes, decay_rates, direct_weight, norm_gain, routes, segments,
):
    tok, width = tokens.shape[1:]
    heads = decay_rates.shape[0] // 2
    blocks = tok // BLOCK
    half = width // 2
    chunks = half // LANES
    n = STATE_ENTRIES
    f32, bf16 = jnp.float32, jnp.bfloat16

    targets = routes[0, :, 0]
    order = jnp.arange(blocks)
    earlier = order[:, None] > order[None, :]
    rank = jnp.sum((targets[:, None] == targets[None, :]) & earlier, axis=1)
    row = jnp.broadcast_to(targets[:, None], (blocks, BLOCK)).reshape(1, tok)
    slot = (rank[:, None] * BLOCK + jnp.arange(BLOCK)[None, :]).reshape(1, tok)
    meta = jnp.concatenate(
        [row, slot, segments.reshape(2, tok), jnp.zeros((4, tok), jnp.int32)], 0
    ).astype(f32)
    dt = step_sizes.reshape(blocks, 2, heads, BLOCK).transpose(1, 2, 0, 3).reshape(2, heads, tok)
    by_head = jnp.stack([decay_rates.reshape(2, heads), direct_weight.reshape(2, heads)], 1)
    by_head = jnp.pad(by_head, ((0, 0), (0, 6), (0, LANES - heads)))
    dma = pltpu.SemaphoreType.DMA
    vmem = pltpu.VMEM
    y, scale = pl.pallas_call(
        functools.partial(kernel, n_phase, n_tensor, float(n_tensor * width)),
        out_shape=[
            jax.ShapeDtypeStruct((tok, width), bf16),
            jax.ShapeDtypeStruct((8, tok), f32),
        ],
        in_specs=[pl.BlockSpec(memory_space=pltpu.HBM)]
        + [pl.BlockSpec(memory_space=pltpu.VMEM)] * 4,
        out_specs=[pl.BlockSpec(memory_space=pltpu.VMEM)] * 2,
        scratch_shapes=[
            vmem((2 * tok, half), bf16),
            vmem((2 * tok, 2 * n), bf16),
            vmem((2, heads, tok), bf16),
            vmem((2, 8, tok), f32),
            vmem((2, 8, tok), f32),
            vmem((chunks, 2 * n, LANES), f32),
            vmem((2 * tok, half), bf16),
            vmem((chunks, 2 * n, LANES), bf16),
            vmem((chunks, 2 * n, LANES), bf16),
            vmem((chunks, 2 * tok, LANES), bf16),
            vmem((tok, width), bf16),
            vmem((n_tensor - 1, 8, tok), f32),
            vmem((8, tok), f32),
            dma((3,)), dma((3,)), dma, dma, dma((2,)), dma((2,)),
            dma((chunks,)), dma((chunks,)), dma((2 * chunks,)), dma((2 * chunks,)),
            dma((chunks,)), dma((chunks,)), dma((n_tensor - 1,)), dma((n_tensor - 1,)), dma,
        ],
        compiler_params=pltpu.CompilerParams(
            collective_id=0, has_side_effects=True, vmem_limit_bytes=40 * 2**20
        ),
    )(tokens.reshape(tok, width), bc_proj.reshape(tok, -1), dt, by_head, meta)
    mixed = y.astype(f32) * scale[0][:, None] * norm_gain[None, :]
    return mixed.astype(bf16).reshape(1, tok, width)


def solution(mesh):
    return jax.shard_map(
        functools.partial(per_device, mesh.shape["phase"], mesh.shape["tensor"]),
        mesh=mesh,
        in_specs=(
            P("dp", "phase", "tensor"),
            P("dp", "phase", None, "tensor"),
            P("dp", "phase", "tensor"),
            P("tensor"),
            P("tensor"),
            P("tensor"),
            P("dp", "phase", None),
            P("dp", "phase"),
        ),
        out_specs=P("dp", "phase", "tensor"),
        check_vma=False,
    )
```

```python
import functools

import jax
import jax.numpy as jnp
from jax import lax
from jax.experimental import pallas as pl
from jax.experimental.pallas import tpu as pltpu
from jax.sharding import PartitionSpec as P

HEAD_FEATURES = 64
STATE_ENTRIES = 256
BLOCK = 8
EPSILON = 1e-05
LANES = 128
WINDOW = 3
ROW_KEY = 1024.0
MESH = pl.DeviceIdType.MESH


def kernel(
    n_phase, n_tensor, total_features,
    x_ref, bc_ref, dt_ref, decay_ref, direct_ref, routes_ref, seg_ref,
    y_ref, scale_ref,
    xall, bcall, dtall, mymeta, meta, metaprev, local, xscaled, hin, hout, ysend, ymine, sums, mysum,
    s_meta, r_meta, s_dt, r_dt, s_bc, r_bc, s_x, r_x, s_h, r_h, s_y, r_y, s_sum, r_sum, s_own,
):
    f32, bf16 = jnp.float32, jnp.bfloat16
    me, phase, place = lax.axis_index("dp"), lax.axis_index("phase"), lax.axis_index("tensor")
    other = 1 - me
    tok, width = x_ref.shape
    half = width // 2
    chunks = half // LANES
    n = STATE_ENTRIES
    blocks = dt_ref.shape[0]
    heads = decay_ref.shape[1] // 2
    lanes_dt = heads * BLOCK
    partner = (other, phase, place)
    first = phase == 0

    my_rows = pl.ds(pl.multiple_of(me * tok, tok), tok)
    other_rows = pl.ds(pl.multiple_of(other * tok, tok), tok)
    my_group = pl.ds(pl.multiple_of(me * n, n), n)
    other_group = pl.ds(pl.multiple_of(other * n, n), n)
    my_c = pl.ds(pl.multiple_of(2 * n + me * n, n), n)
    other_c = pl.ds(pl.multiple_of(2 * n + other * n, n), n)
    own_x = pltpu.make_async_copy(
        x_ref.at[:, pl.ds(pl.multiple_of(me * half, half), half)], xall.at[my_rows], s_own
    )
    own_x.start()

    token_block = lax.broadcasted_iota(jnp.int32, (blocks, tok), 1) // BLOCK
    widen = jnp.where(token_block == lax.broadcasted_iota(jnp.int32, (blocks, tok), 0), 1.0, 0.0)
    own_rows = jnp.dot(
        jnp.broadcast_to(routes_ref[...].astype(f32), (8, blocks)).astype(bf16),
        widen.astype(bf16), preferred_element_type=f32,
    )
    mymeta[...] = own_rows
    for j in range(2):
        mymeta[2 + j : 3 + j, :] = seg_ref[0:1, j * tok : (j + 1) * tok].astype(f32)

    barrier = pltpu.get_barrier_semaphore()
    pl.semaphore_signal(barrier, inc=1, device_id=partner, device_id_type=MESH)
    for k in range(1, n_tensor):
        pl.semaphore_signal(
            barrier, inc=1, device_id=(me, phase, lax.rem(place + k, n_tensor)), device_id_type=MESH
        )

    @pl.when(phase > 0)
    def _():
        for d in (me, other):
            pl.semaphore_signal(barrier, inc=1, device_id=(d, phase - 1, place), device_id_type=MESH)

    @pl.when(phase < n_phase - 1)
    def _():
        for d in (me, other):
            pl.semaphore_signal(barrier, inc=1, device_id=(d, phase + 1, place), device_id_type=MESH)

    peers = n_tensor + 2 * jnp.minimum(phase, 1) + 2 * jnp.minimum(n_phase - 1 - phase, 1)
    pl.semaphore_wait(barrier, peers)

    def remote(src, dst, send, recv, device):
        return pltpu.make_async_remote_copy(
            src_ref=src, dst_ref=dst, send_sem=send, recv_sem=recv,
            device_id=device, device_id_type=MESH,
        )

    copies = [
        remote(mymeta, meta.at[me], s_meta.at[0], r_meta.at[0], partner),
        remote(
            dt_ref.at[:, pl.ds(pl.multiple_of(other * lanes_dt, LANES), lanes_dt)],
            dtall.at[me], s_dt, r_dt, partner,
        ),
        remote(bc_ref.at[:, other_group], bcall.at[my_rows, pl.ds(0, n)], s_bc.at[0], r_bc.at[0], partner),
        remote(bc_ref.at[:, other_c], bcall.at[my_rows, pl.ds(n, n)], s_bc.at[1], r_bc.at[1], partner),
    ]
    x_copies = [
        remote(
            x_ref.at[:, pl.ds(pl.multiple_of(other * half + c * LANES, LANES), LANES)],
            xall.at[my_rows, pl.ds(c * LANES, LANES)],
            s_x.at[c], r_x.at[c], partner,
        )
        for c in range(chunks)
    ]
    after = jnp.minimum(phase + 1, n_phase - 1)
    ahead = [
        remote(mymeta, metaprev.at[me], s_meta.at[1 + i], r_meta.at[1 + i], (d, after, place))
        for i, d in enumerate((me, other))
    ]
    h_copies = [
        [
            remote(
                hout.at[c, pl.ds(d * n, n)], hin.at[c, pl.ds(d * n, n)],
                s_h.at[2 * c + d], r_h.at[2 * c + d], (me, after, place),
            )
            for d in range(2)
        ]
        for c in range(chunks)
    ]
    queue = x_copies + copies[3:]
    for copy in copies[:3] + queue[:2]:
        copy.start()

    @pl.when(phase < n_phase - 1)
    def _():
        for copy in ahead:
            copy.start()

    meta[me] = mymeta[...]
    dtall[me] = dt_ref[:, pl.ds(pl.multiple_of(me * lanes_dt, LANES), lanes_dt)]
    bcall[my_rows, pl.ds(0, n)] = bc_ref[:, my_group]
    bcall[my_rows, pl.ds(n, n)] = bc_ref[:, my_c]

    @pl.when(first)
    def _():
        metaprev[...] = jnp.full_like(metaprev, -(2.0**20))
        hin[...] = jnp.zeros_like(hin)

    both = 2 * tok
    at_row = lax.broadcasted_iota(jnp.int32, (both, both), 0)
    at_col = lax.broadcasted_iota(jnp.int32, (both, both), 1)
    causal = at_row >= at_col
    tok_row = lax.broadcasted_iota(jnp.int32, (tok, tok), 0)
    tok_col = lax.broadcasted_iota(jnp.int32, (tok, tok), 1)
    before = tok_row // BLOCK < tok_col // BLOCK
    inner = (tok_col % BLOCK)[0:1].astype(f32)
    widen_t = jnp.where(
        lax.broadcasted_iota(jnp.int32, (tok, blocks), 0) // BLOCK
        == lax.broadcasted_iota(jnp.int32, (tok, blocks), 1),
        1.0, 0.0,
    ).astype(bf16)
    same_place = (
        lax.broadcasted_iota(jnp.int32, (tok, lanes_dt), 0) % BLOCK
        == lax.broadcasted_iota(jnp.int32, (tok, lanes_dt), 1) % BLOCK
    )
    gather_head = jnp.where(
        lax.broadcasted_iota(jnp.int32, (lanes_dt, LANES), 0) // BLOCK
        == lax.broadcasted_iota(jnp.int32, (lanes_dt, LANES), 1),
        1.0, 0.0,
    ).astype(bf16)
    slots = tok_row.astype(f32)

    copies[0].wait_recv()

    row_lanes, key_lanes, row_subl, key_subl = [], [], [], []
    for j in range(2):
        rows = meta[j, 0:1, :]
        rows_t = jnp.broadcast_to(rows, (tok, tok)).T
        count = jnp.dot(
            jnp.ones((8, tok), bf16),
            jnp.where(before & (rows_t == rows), 1.0, 0.0).astype(bf16),
            preferred_element_type=f32,
        )
        places = jnp.where(slots == count[0:1] + inner, 1.0, 0.0).astype(bf16)
        found = [
            jnp.dot(meta[d].astype(bf16), places, preferred_element_type=f32)[2 + j : 3 + j, :]
            for d in range(2)
        ]
        key = rows * ROW_KEY + jnp.where(rows == 0.0, found[0], found[1])
        row_lanes.append(rows)
        key_lanes.append(key)
        row_subl.append(rows_t)
        key_subl.append(jnp.broadcast_to(key, (tok, tok)).T)
    row_lane, key_lane = jnp.concatenate(row_lanes, 1), jnp.concatenate(key_lanes, 1)
    row_sub, key_sub = jnp.concatenate(row_subl, 0), jnp.concatenate(key_subl, 0)
    row_sub2 = jnp.concatenate([row_sub, row_sub], 1)
    key_sub2 = jnp.concatenate([key_sub, key_sub], 1)
    same_row = jnp.where(causal & (row_sub2 == row_lane), 1.0, 0.0).astype(bf16)
    picks = jnp.where(
        lax.broadcasted_iota(jnp.int32, (16, both), 0).astype(f32) == row_lane, 1.0, 0.0
    ).astype(bf16)
    ends = [meta[d, 3:4, tok - 1 : tok] for d in range(2)]

    copies[1].wait_recv()
    decay, direct_w = [
        jnp.concatenate(
            [
                jnp.where(me == 0, ref[0:1, 0:heads], ref[0:1, heads : 2 * heads]),
                jnp.zeros((1, LANES - heads), f32),
            ],
            1,
        )
        for ref in (decay_ref, direct_ref)
    ]
    dt_parts = []
    for j in range(2):
        wide = jnp.dot(widen_t, dtall[j], preferred_element_type=f32)
        wide = jnp.where(same_place, wide, 0.0).astype(bf16)
        dt_parts.append(jnp.dot(wide, gather_head, preferred_element_type=f32))
    dt = jnp.concatenate(dt_parts, 0)
    steps = jnp.dot(
        jnp.concatenate([same_row, picks], 0), dt.astype(bf16), preferred_element_type=f32
    )
    log_decay = -decay * steps[0:both]
    grow = jnp.exp(-log_decay) * dt
    shrink = jnp.exp(log_decay)
    whole = jnp.exp(-decay * steps[both : both + 8])

    copies[2].wait_recv()
    queue[2].start()
    b_mat = bcall[:, 0:n]
    b_float = b_mat.astype(f32)
    b_both_t = jnp.concatenate(
        [
            jnp.where(key_sub2 == ends[d] + d * ROW_KEY, b_float, 0.0).T.astype(bf16)
            for d in range(2)
        ],
        0,
    )

    def spread(a, c):
        low = lax.broadcasted_iota(jnp.int32, (a.shape[0], LANES), 1) < HEAD_FEATURES
        shape = (a.shape[0], LANES)
        return jnp.where(
            low,
            jnp.broadcast_to(a[:, 2 * c : 2 * c + 1], shape),
            jnp.broadcast_to(a[:, 2 * c + 1 : 2 * c + 2], shape),
        )

    pieces = [copy for pair in h_copies for copy in pair]
    own_x.wait()
    for c in range(chunks):
        x_copies[c].wait_recv()
        if c + 3 < len(queue):
            queue[c + 3].start()
        cols = pl.ds(c * LANES, LANES)
        scaled = (xall[:, cols].astype(f32) * spread(grow, c)).astype(bf16)
        xscaled[:, cols] = scaled
        keep = spread(whole, c)
        update = jnp.dot(b_both_t, scaled, preferred_element_type=f32)
        update = jnp.concatenate(
            [update[d * n : (d + 1) * n] * keep[d : d + 1] for d in range(2)], 0
        )

        @pl.when(first)
        def _():
            hout[c] = update.astype(bf16)
            for d in range(2):
                if 2 * c + d >= WINDOW:
                    pieces[2 * c + d - WINDOW].wait_send()
                h_copies[c][d].start()

        @pl.when(phase > 0)
        def _():
            local[c] = update

    @pl.when(phase > 0)
    def _():
        for copy in ahead:
            copy.wait_recv()

    befores = [metaprev[d, 3:4, tok - 1 : tok] for d in range(2)]
    through = [jnp.where(ends[d] == befores[d], 1.0, 0.0) for d in range(2)]
    copies[3].wait_recv()
    c_mat = bcall[:, n : 2 * n]
    c_float = c_mat.astype(f32)
    c_both = jnp.concatenate(
        [
            jnp.where(key_sub2 == befores[d] + d * ROW_KEY, c_float, 0.0).astype(bf16)
            for d in range(2)
        ],
        1,
    )
    scores = lax.dot_general(c_mat, b_mat, (((1,), (1,)), ((), ())), preferred_element_type=f32)
    scores = jnp.where(causal & (key_sub2 == key_lane), scores, 0.0).astype(bf16)

    squares = jnp.zeros((tok, LANES), f32)
    y_copies = []
    for c in range(chunks):
        cols = pl.ds(c * LANES, LANES)
        inside = jnp.dot(scores, xscaled[:, cols], preferred_element_type=f32)
        decayed = spread(shrink, c)
        direct = spread(direct_w, c) * xall[:, cols].astype(f32)
        keep = spread(whole, c)
        for d in range(2):
            rows = pl.ds(d * n, n)

            @pl.when(phase > 0)
            def _():
                h_copies[c][d].wait_recv()

            @pl.when((phase > 0) & (phase < n_phase - 1))
            def _():
                hout[c, rows, :] = (
                    local[c, rows, :] + (keep[d : d + 1] * through[d]) * hin[c, rows, :].astype(f32)
                ).astype(bf16)
                h_copies[c][d].start()

        carried = jnp.dot(c_both, hin[c], preferred_element_type=f32)
        ysend[c] = (decayed * (inside + carried) + direct).astype(bf16)
        here = pl.ds(pl.multiple_of(me * half + c * LANES, LANES), LANES)
        copy = remote(ysend.at[c, other_rows], ymine.at[:, here], s_y.at[c], r_y.at[c], partner)
        copy.start()
        y_copies.append(copy)
        own = ysend[c, my_rows]
        y_ref[:, here] = own
        own = own.astype(f32)
        squares = squares + own * own

    for c in range(chunks):
        y_copies[c].wait_recv()
        there = pl.ds(pl.multiple_of(other * half + c * LANES, LANES), LANES)
        got = ymine[:, there]
        y_ref[:, there] = got
        got = got.astype(f32)
        squares = squares + got * got

    per_token = jnp.broadcast_to(jnp.sum(squares, axis=1, keepdims=True), (tok, tok)).T[0:8, :]
    mysum[...] = per_token
    sum_copies = []
    for k in range(1, n_tensor):
        copy = remote(
            mysum, sums.at[k - 1], s_sum.at[k - 1], r_sum.at[k - 1],
            (me, phase, lax.rem(place + k, n_tensor)),
        )
        copy.start()
        sum_copies.append(copy)
    total = per_token
    for copy in copies + x_copies + y_copies:
        copy.wait_send()

    @pl.when(phase < n_phase - 1)
    def _():
        for copy in ahead + pieces[-WINDOW:]:
            copy.wait_send()

    @pl.when((phase > 0) & (phase < n_phase - 1))
    def _():
        for copy in pieces[:-WINDOW]:
            copy.wait_send()

    for k in range(1, n_tensor):
        sum_copies[k - 1].wait_recv()
        total = total + sums[k - 1]
    scale_ref[...] = lax.rsqrt(total / total_features + EPSILON)
    for copy in sum_copies:
        copy.wait_send()


def per_device(
    n_phase, n_tensor,
    tokens, bc_proj, step_sizes, decay_rates, direct_weight, norm_gain, routes, segments,
):
    tok, width = tokens.shape[1:]
    heads = decay_rates.shape[0] // 2
    blocks = tok // BLOCK
    half = width // 2
    chunks = half // LANES
    n = STATE_ENTRIES
    f32, bf16 = jnp.float32, jnp.bfloat16

    dma = pltpu.SemaphoreType.DMA
    vmem = pltpu.VMEM
    y, scale = pl.pallas_call(
        functools.partial(kernel, n_phase, n_tensor, float(n_tensor * width)),
        out_shape=[
            jax.ShapeDtypeStruct((tok, width), bf16),
            jax.ShapeDtypeStruct((8, tok), f32),
        ],
        in_specs=[pl.BlockSpec(memory_space=pltpu.HBM)]
        + [pl.BlockSpec(memory_space=pltpu.VMEM)] * 6,
        out_specs=[pl.BlockSpec(memory_space=pltpu.VMEM)] * 2,
        scratch_shapes=[
            vmem((2 * tok, half), bf16),
            vmem((2 * tok, 2 * n), bf16),
            vmem((2, blocks, heads * BLOCK), bf16),
            vmem((8, tok), f32),
            vmem((2, 8, tok), f32),
            vmem((2, 8, tok), f32),
            vmem((chunks, 2 * n, LANES), f32),
            vmem((2 * tok, half), bf16),
            vmem((chunks, 2 * n, LANES), bf16),
            vmem((chunks, 2 * n, LANES), bf16),
            vmem((chunks, 2 * tok, LANES), bf16),
            vmem((tok, width), bf16),
            vmem((n_tensor - 1, 8, tok), f32),
            vmem((8, tok), f32),
            dma((3,)), dma((3,)), dma, dma, dma((2,)), dma((2,)),
            dma((chunks,)), dma((chunks,)), dma((2 * chunks,)), dma((2 * chunks,)),
            dma((chunks,)), dma((chunks,)), dma((n_tensor - 1,)), dma((n_tensor - 1,)), dma,
        ],
        compiler_params=pltpu.CompilerParams(
            collective_id=0, has_side_effects=True, vmem_limit_bytes=40 * 2**20
        ),
    )(
        tokens.reshape(tok, width), bc_proj.reshape(tok, -1), step_sizes.reshape(blocks, -1),
        decay_rates.reshape(1, -1), direct_weight.reshape(1, -1), routes.reshape(1, -1), segments,
    )
    mixed = y.astype(f32) * scale[0][:, None] * norm_gain[None, :]
    return mixed.astype(bf16).reshape(1, tok, width)


def solution(mesh):
    return jax.shard_map(
        functools.partial(per_device, mesh.shape["phase"], mesh.shape["tensor"]),
        mesh=mesh,
        in_specs=(
            P("dp", "phase", "tensor"),
            P("dp", "phase", None, "tensor"),
            P("dp", "phase", "tensor"),
            P("tensor"),
            P("tensor"),
            P("tensor"),
            P("dp", "phase", None),
            P("dp", "phase"),
        ),
        out_specs=P("dp", "phase", "tensor"),
        check_vma=False,
    )
```

```python
import functools

import jax
import jax.numpy as jnp
from jax import lax
from jax.experimental import pallas as pl
from jax.experimental.pallas import tpu as pltpu
from jax.sharding import PartitionSpec as P

HEAD_FEATURES = 64
STATE_ENTRIES = 256
BLOCK = 8
EPSILON = 1e-05
LANES = 128
WINDOW = 3
ROW_KEY = 1024.0
MESH = pl.DeviceIdType.MESH


def kernel(
    n_phase, n_tensor, total_features,
    x_ref, bc_ref, dt_ref, decay_ref, direct_ref, routes_ref, seg_ref,
    y_ref, scale_ref,
    xall, bcall, dtall, mymeta, meta, metaprev, local, xscaled, hin, hout, ysend, ymine, sums, mysum,
    s_meta, r_meta, s_dt, r_dt, s_bc, r_bc, s_x, r_x, s_h, r_h, s_y, r_y, s_sum, r_sum, s_own,
):
    f32, bf16 = jnp.float32, jnp.bfloat16
    me, phase, place = lax.axis_index("dp"), lax.axis_index("phase"), lax.axis_index("tensor")
    other = 1 - me
    tok, width = x_ref.shape
    half = width // 2
    chunks = half // LANES
    n = STATE_ENTRIES
    blocks = dt_ref.shape[0]
    heads = decay_ref.shape[1] // 2
    lanes_dt = heads * BLOCK
    partner = (other, phase, place)
    first = phase == 0

    my_rows = pl.ds(pl.multiple_of(me * tok, tok), tok)
    other_rows = pl.ds(pl.multiple_of(other * tok, tok), tok)
    my_group = pl.ds(pl.multiple_of(me * n, n), n)
    other_group = pl.ds(pl.multiple_of(other * n, n), n)
    my_c = pl.ds(pl.multiple_of(2 * n + me * n, n), n)
    other_c = pl.ds(pl.multiple_of(2 * n + other * n, n), n)
    own_x = pltpu.make_async_copy(
        x_ref.at[:, pl.ds(pl.multiple_of(me * half, half), half)], xall.at[my_rows], s_own
    )
    own_x.start()

    token_block = lax.broadcasted_iota(jnp.int32, (blocks, tok), 1) // BLOCK
    widen = jnp.where(token_block == lax.broadcasted_iota(jnp.int32, (blocks, tok), 0), 1.0, 0.0)
    own_rows = jnp.dot(
        jnp.broadcast_to(routes_ref[...].astype(f32), (8, blocks)).astype(bf16),
        widen.astype(bf16), preferred_element_type=f32,
    )
    mymeta[...] = own_rows
    for j in range(2):
        mymeta[2 + j : 3 + j, :] = seg_ref[0:1, j * tok : (j + 1) * tok].astype(f32)

    barrier = pltpu.get_barrier_semaphore()
    pl.semaphore_signal(barrier, inc=1, device_id=partner, device_id_type=MESH)
    for k in range(1, n_tensor):
        pl.semaphore_signal(
            barrier, inc=1, device_id=(me, phase, lax.rem(place + k, n_tensor)), device_id_type=MESH
        )

    @pl.when(phase > 0)
    def _():
        for d in (me, other):
            pl.semaphore_signal(barrier, inc=1, device_id=(d, phase - 1, place), device_id_type=MESH)

    @pl.when(phase < n_phase - 1)
    def _():
        for d in (me, other):
            pl.semaphore_signal(barrier, inc=1, device_id=(d, phase + 1, place), device_id_type=MESH)

    peers = n_tensor + 2 * jnp.minimum(phase, 1) + 2 * jnp.minimum(n_phase - 1 - phase, 1)
    pl.semaphore_wait(barrier, peers)

    def remote(src, dst, send, recv, device):
        return pltpu.make_async_remote_copy(
            src_ref=src, dst_ref=dst, send_sem=send, recv_sem=recv,
            device_id=device, device_id_type=MESH,
        )

    copies = [
        remote(mymeta, meta.at[me], s_meta.at[0], r_meta.at[0], partner),
        remote(
            dt_ref.at[:, pl.ds(pl.multiple_of(other * lanes_dt, LANES), lanes_dt)],
            dtall.at[me], s_dt, r_dt, partner,
        ),
        remote(bc_ref.at[:, other_group], bcall.at[my_rows, pl.ds(0, n)], s_bc.at[0], r_bc.at[0], partner),
        remote(bc_ref.at[:, other_c], bcall.at[my_rows, pl.ds(n, n)], s_bc.at[1], r_bc.at[1], partner),
    ]
    x_copies = [
        remote(
            x_ref.at[:, pl.ds(pl.multiple_of(other * half + c * LANES, LANES), LANES)],
            xall.at[my_rows, pl.ds(c * LANES, LANES)],
            s_x.at[c], r_x.at[c], partner,
        )
        for c in range(chunks)
    ]
    after = jnp.minimum(phase + 1, n_phase - 1)
    ahead = [
        remote(mymeta, metaprev.at[me], s_meta.at[1 + i], r_meta.at[1 + i], (d, after, place))
        for i, d in enumerate((me, other))
    ]
    h_copies = [
        [
            remote(
                hout.at[c, pl.ds(d * n, n)], hin.at[c, pl.ds(d * n, n)],
                s_h.at[2 * c + d], r_h.at[2 * c + d], (me, after, place),
            )
            for d in range(2)
        ]
        for c in range(chunks)
    ]
    queue = x_copies[:2] + copies[3:] + x_copies[2:]
    for copy in copies[:3] + queue[:2]:
        copy.start()

    @pl.when(phase < n_phase - 1)
    def _():
        for copy in ahead:
            copy.start()

    meta[me] = mymeta[...]
    dtall[me] = dt_ref[:, pl.ds(pl.multiple_of(me * lanes_dt, LANES), lanes_dt)]
    bcall[my_rows, pl.ds(0, n)] = bc_ref[:, my_group]
    bcall[my_rows, pl.ds(n, n)] = bc_ref[:, my_c]

    @pl.when(first)
    def _():
        metaprev[...] = jnp.full_like(metaprev, -(2.0**20))
        hin[...] = jnp.zeros_like(hin)

    both = 2 * tok
    at_row = lax.broadcasted_iota(jnp.int32, (both, both), 0)
    at_col = lax.broadcasted_iota(jnp.int32, (both, both), 1)
    causal = at_row >= at_col
    tok_row = lax.broadcasted_iota(jnp.int32, (tok, tok), 0)
    tok_col = lax.broadcasted_iota(jnp.int32, (tok, tok), 1)
    before = tok_row // BLOCK < tok_col // BLOCK
    inner = (tok_col % BLOCK)[0:1].astype(f32)
    widen_t = jnp.where(
        lax.broadcasted_iota(jnp.int32, (tok, blocks), 0) // BLOCK
        == lax.broadcasted_iota(jnp.int32, (tok, blocks), 1),
        1.0, 0.0,
    ).astype(bf16)
    same_place = (
        lax.broadcasted_iota(jnp.int32, (tok, lanes_dt), 0) % BLOCK
        == lax.broadcasted_iota(jnp.int32, (tok, lanes_dt), 1) % BLOCK
    )
    gather_head = jnp.where(
        lax.broadcasted_iota(jnp.int32, (lanes_dt, LANES), 0) // BLOCK
        == lax.broadcasted_iota(jnp.int32, (lanes_dt, LANES), 1),
        1.0, 0.0,
    ).astype(bf16)
    slots = tok_row.astype(f32)

    copies[0].wait_recv()

    row_lanes, key_lanes, row_subl, key_subl = [], [], [], []
    for j in range(2):
        rows = meta[j, 0:1, :]
        rows_t = jnp.broadcast_to(rows, (tok, tok)).T
        count = jnp.dot(
            jnp.ones((8, tok), bf16),
            jnp.where(before & (rows_t == rows), 1.0, 0.0).astype(bf16),
            preferred_element_type=f32,
        )
        places = jnp.where(slots == count[0:1] + inner, 1.0, 0.0).astype(bf16)
        found = [
            jnp.dot(meta[d].astype(bf16), places, preferred_element_type=f32)[2 + j : 3 + j, :]
            for d in range(2)
        ]
        key = rows * ROW_KEY + jnp.where(rows == 0.0, found[0], found[1])
        row_lanes.append(rows)
        key_lanes.append(key)
        row_subl.append(rows_t)
        key_subl.append(jnp.broadcast_to(key, (tok, tok)).T)
    row_lane, key_lane = jnp.concatenate(row_lanes, 1), jnp.concatenate(key_lanes, 1)
    row_sub, key_sub = jnp.concatenate(row_subl, 0), jnp.concatenate(key_subl, 0)
    row_sub2 = jnp.concatenate([row_sub, row_sub], 1)
    key_sub2 = jnp.concatenate([key_sub, key_sub], 1)
    same_row = jnp.where(causal & (row_sub2 == row_lane), 1.0, 0.0).astype(bf16)
    picks = jnp.where(
        lax.broadcasted_iota(jnp.int32, (16, both), 0).astype(f32) == row_lane, 1.0, 0.0
    ).astype(bf16)
    ends = [meta[d, 3:4, tok - 1 : tok] for d in range(2)]

    copies[1].wait_recv()
    decay, direct_w = [
        jnp.concatenate(
            [
                jnp.where(me == 0, ref[0:1, 0:heads], ref[0:1, heads : 2 * heads]),
                jnp.zeros((1, LANES - heads), f32),
            ],
            1,
        )
        for ref in (decay_ref, direct_ref)
    ]
    dt_parts = []
    for j in range(2):
        wide = jnp.dot(widen_t, dtall[j], preferred_element_type=f32)
        wide = jnp.where(same_place, wide, 0.0).astype(bf16)
        dt_parts.append(jnp.dot(wide, gather_head, preferred_element_type=f32))
    dt = jnp.concatenate(dt_parts, 0)
    steps = jnp.dot(
        jnp.concatenate([same_row, picks], 0), dt.astype(bf16), preferred_element_type=f32
    )
    log_decay = -decay * steps[0:both]
    grow = jnp.exp(-log_decay) * dt
    shrink = jnp.exp(log_decay)
    whole = jnp.exp(-decay * steps[both : both + 8])

    copies[2].wait_recv()
    queue[2].start()
    queue[3].start()
    b_mat = bcall[:, 0:n]
    b_float = b_mat.astype(f32)
    b_both_t = jnp.concatenate(
        [
            jnp.where(key_sub2 == ends[d] + d * ROW_KEY, b_float, 0.0).T.astype(bf16)
            for d in range(2)
        ],
        0,
    )

    def spread(a, c):
        low = lax.broadcasted_iota(jnp.int32, (a.shape[0], LANES), 1) < HEAD_FEATURES
        shape = (a.shape[0], LANES)
        return jnp.where(
            low,
            jnp.broadcast_to(a[:, 2 * c : 2 * c + 1], shape),
            jnp.broadcast_to(a[:, 2 * c + 1 : 2 * c + 2], shape),
        )

    pieces = [copy for pair in h_copies for copy in pair]

    @pl.when(phase > 0)
    def _():
        for copy in ahead:
            copy.wait_recv()

    befores = [metaprev[d, 3:4, tok - 1 : tok] for d in range(2)]
    through = [jnp.where(ends[d] == befores[d], 1.0, 0.0) for d in range(2)]
    own_x.wait()

    def mixers():
        copies[3].wait_recv()
        c_mat = bcall[:, n : 2 * n]
        c_float = c_mat.astype(f32)
        c_both = jnp.concatenate(
            [
                jnp.where(key_sub2 == befores[d] + d * ROW_KEY, c_float, 0.0).astype(bf16)
                for d in range(2)
            ],
            1,
        )
        scores = lax.dot_general(c_mat, b_mat, (((1,), (1,)), ((), ())), preferred_element_type=f32)
        scores = jnp.where(causal & (key_sub2 == key_lane), scores, 0.0).astype(bf16)
        return scores, c_both

    def output(c, scores, c_both, squares):
        cols = pl.ds(c * LANES, LANES)
        inside = jnp.dot(scores, xscaled[:, cols], preferred_element_type=f32)
        carried = jnp.dot(c_both, hin[c], preferred_element_type=f32)
        direct = spread(direct_w, c) * xall[:, cols].astype(f32)
        ysend[c] = (spread(shrink, c) * (inside + carried) + direct).astype(bf16)
        here = pl.ds(pl.multiple_of(me * half + c * LANES, LANES), LANES)
        copy = remote(ysend.at[c, other_rows], ymine.at[:, here], s_y.at[c], r_y.at[c], partner)
        copy.start()
        y_copies.append(copy)
        own = ysend[c, my_rows]
        y_ref[:, here] = own
        own = own.astype(f32)
        return squares + own * own

    squares = jnp.zeros((tok, LANES), f32)
    y_copies = []
    scores = c_both = None
    for c in range(chunks):
        x_copies[c].wait_recv()
        if c + 4 < len(queue):
            queue[c + 4].start()
        cols = pl.ds(c * LANES, LANES)
        scaled = (xall[:, cols].astype(f32) * spread(grow, c)).astype(bf16)
        xscaled[:, cols] = scaled
        keep = spread(whole, c)
        update = jnp.dot(b_both_t, scaled, preferred_element_type=f32)
        update = jnp.concatenate(
            [update[d * n : (d + 1) * n] * keep[d : d + 1] for d in range(2)], 0
        )

        @pl.when(first)
        def _():
            hout[c] = update.astype(bf16)
            for d in range(2):
                if 2 * c + d >= WINDOW:
                    pieces[2 * c + d - WINDOW].wait_send()
                h_copies[c][d].start()

        @pl.when((phase > 0) & (phase < n_phase - 1))
        def _():
            local[c] = update

        if c == 1:
            scores, c_both = mixers()
        if c > 0:
            squares = output(c - 1, scores, c_both, squares)
        for d in range(2):
            rows = pl.ds(d * n, n)

            @pl.when(phase > 0)
            def _():
                h_copies[c][d].wait_recv()

            @pl.when((phase > 0) & (phase < n_phase - 1))
            def _():
                hout[c, rows, :] = (
                    local[c, rows, :] + (keep[d : d + 1] * through[d]) * hin[c, rows, :].astype(f32)
                ).astype(bf16)
                h_copies[c][d].start()

    squares = output(chunks - 1, scores, c_both, squares)

    for c in range(chunks):
        y_copies[c].wait_recv()
        there = pl.ds(pl.multiple_of(other * half + c * LANES, LANES), LANES)
        got = ymine[:, there]
        y_ref[:, there] = got
        got = got.astype(f32)
        squares = squares + got * got

    per_token = jnp.broadcast_to(jnp.sum(squares, axis=1, keepdims=True), (tok, tok)).T[0:8, :]
    mysum[...] = per_token
    sum_copies = []
    for k in range(1, n_tensor):
        copy = remote(
            mysum, sums.at[k - 1], s_sum.at[k - 1], r_sum.at[k - 1],
            (me, phase, lax.rem(place + k, n_tensor)),
        )
        copy.start()
        sum_copies.append(copy)
    total = per_token
    for copy in copies + x_copies + y_copies:
        copy.wait_send()

    @pl.when(phase < n_phase - 1)
    def _():
        for copy in ahead + pieces[-WINDOW:]:
            copy.wait_send()

    @pl.when((phase > 0) & (phase < n_phase - 1))
    def _():
        for copy in pieces[:-WINDOW]:
            copy.wait_send()

    for k in range(1, n_tensor):
        sum_copies[k - 1].wait_recv()
        total = total + sums[k - 1]
    scale_ref[...] = lax.rsqrt(total / total_features + EPSILON)
    for copy in sum_copies:
        copy.wait_send()


def per_device(
    n_phase, n_tensor,
    tokens, bc_proj, step_sizes, decay_rates, direct_weight, norm_gain, routes, segments,
):
    tok, width = tokens.shape[1:]
    heads = decay_rates.shape[0] // 2
    blocks = tok // BLOCK
    half = width // 2
    chunks = half // LANES
    n = STATE_ENTRIES
    f32, bf16 = jnp.float32, jnp.bfloat16

    dma = pltpu.SemaphoreType.DMA
    vmem = pltpu.VMEM
    y, scale = pl.pallas_call(
        functools.partial(kernel, n_phase, n_tensor, float(n_tensor * width)),
        out_shape=[
            jax.ShapeDtypeStruct((tok, width), bf16),
            jax.ShapeDtypeStruct((8, tok), f32),
        ],
        in_specs=[pl.BlockSpec(memory_space=pltpu.HBM)]
        + [pl.BlockSpec(memory_space=pltpu.VMEM)] * 6,
        out_specs=[pl.BlockSpec(memory_space=pltpu.VMEM)] * 2,
        scratch_shapes=[
            vmem((2 * tok, half), bf16),
            vmem((2 * tok, 2 * n), bf16),
            vmem((2, blocks, heads * BLOCK), bf16),
            vmem((8, tok), f32),
            vmem((2, 8, tok), f32),
            vmem((2, 8, tok), f32),
            vmem((chunks, 2 * n, LANES), f32),
            vmem((2 * tok, half), bf16),
            vmem((chunks, 2 * n, LANES), bf16),
            vmem((chunks, 2 * n, LANES), bf16),
            vmem((chunks, 2 * tok, LANES), bf16),
            vmem((tok, width), bf16),
            vmem((n_tensor - 1, 8, tok), f32),
            vmem((8, tok), f32),
            dma((3,)), dma((3,)), dma, dma, dma((2,)), dma((2,)),
            dma((chunks,)), dma((chunks,)), dma((2 * chunks,)), dma((2 * chunks,)),
            dma((chunks,)), dma((chunks,)), dma((n_tensor - 1,)), dma((n_tensor - 1,)), dma,
        ],
        compiler_params=pltpu.CompilerParams(
            collective_id=0, has_side_effects=True, vmem_limit_bytes=40 * 2**20
        ),
    )(
        tokens.reshape(tok, width), bc_proj.reshape(tok, -1), step_sizes.reshape(blocks, -1),
        decay_rates.reshape(1, -1), direct_weight.reshape(1, -1), routes.reshape(1, -1), segments,
    )
    mixed = y.astype(f32) * scale[0][:, None] * norm_gain[None, :]
    return mixed.astype(bf16).reshape(1, tok, width)


def solution(mesh):
    return jax.shard_map(
        functools.partial(per_device, mesh.shape["phase"], mesh.shape["tensor"]),
        mesh=mesh,
        in_specs=(
            P("dp", "phase", "tensor"),
            P("dp", "phase", None, "tensor"),
            P("dp", "phase", "tensor"),
            P("tensor"),
            P("tensor"),
            P("tensor"),
            P("dp", "phase", None),
            P("dp", "phase"),
        ),
        out_specs=P("dp", "phase", "tensor"),
        check_vma=False,
    )
```
